512 devices in a mesh: blk: 128 (over x_hi, z, y), fld: 4 (over x_lo, core).
Axes of the slice: x: 4 (x_hi: 2, x_lo: 2; x = x_hi * 2 + x_lo), y: 4, z: 16, core: 2. Of those that a mesh axis runs over, the one named last changes fastest.
Arguments:
- coef: bfloat16 [1024, 1280, 256], P(('blk', 'fld')), may hold values from -6 to 6
- leg: bfloat16 [1024, 256, 1280], P(('blk', 'fld')), may hold values from -0.15625 to 0.15625
- vcoef: float32 [4, 7, 32], P('fld'), may hold values from -2.4 to 2.4
- obs_value: bfloat16 [4, 32, 65536], P('fld', None, 'blk'), may hold values from -6 to 6
- obs_weight: float32 [4, 32, 65536], P('fld', None, 'blk'), may hold values from 1 to 10
- obs_dest: int32 [65536, 1], P('blk'), may hold values from 0 to 127; in each aligned block of 512 rows (0 to 511, 512 to 1023, ...) at most 6 rows name the same one
- obs_spot: int32 [65536], P('blk'), may hold values from 0 to 5119
- obs_count: int32 [128], P('blk'), may hold values from 1 to 512, 49280 in all
Outputs:
- obs_gradient: bfloat16 [1024, 1280, 256], P(('blk', 'fld'))
The draws below stay inside these ranges and needn't reach their ends.
Inputs may be any that keep to these rules, and one draw needn't show every extreme that they name: `obs_dest`: in the rows of one index of blk, no band is named more than 6 times, a bound that some block reaches. `obs_count`: some list is full.
All inputs are finite; a program needn't handle non-finite values. No bound on the sum of `obs_count` on one device may be relied on, other than what follows from the above.
Results may differ from the reference program's by a relative error of at most 0.0085.
Values may be sent and summed in bfloat16 or wider, within the bound.
A program may use at most 64 MiB of HBM per device.

```python
import math
import jax
import jax.numpy as jnp
import numpy as np
from jax import lax

NN = 1280
NLON = 2560
FIELDS = 4
LEV = 32
LAT_DEV = 2
HALF = 3
OBS_DEV = 512
M = 1024
NLAT = 256
BAND = 7
OBS_TOTAL = 65536
CAP = 6
N_BLK = 128


def plant(array, stream_key, smallest, high):
    place = [jax.random.randint(jax.random.fold_in(stream_key, axis), (), 0, length) for axis, length in enumerate(array.shape)]
    widest = array.shape.index(max(array.shape))
    next_to = place[:widest] + [(place[widest] + 1) % array.shape[widest]] + place[widest + 1:]
    return array.at[tuple(place)].set(smallest).at[tuple(next_to)].set(high)


def block_scale(stream_key, dims, shards, low, top_value):
    loudness, own = 1.0, jax.random.fold_in(stream_key, 6)
    for dim, shards_of in shards:
        draws = jnp.exp(jax.random.uniform(jax.random.fold_in(own, dim), (shards_of,), jnp.float32, low / len(shards), top_value / len(shards)))
        loudness = loudness * jnp.repeat(draws, dims[dim] // shards_of).reshape([-1 if axis == dim else 1 for axis in range(len(dims))])
    return loudness


def profile(amount, total, most, slope):
    weights = [(1 << 20) // math.isqrt(standing ** slope) + 1 for standing in range(2, amount + 1)]
    surplus, holding = total - most - (amount - 1), [1] * (amount - 1)
    while surplus > 0:
        movable = [i for i in range(amount - 1) if holding[i] < most]
        mass, left = sum([weights[i] for i in movable]), surplus
        for i in movable:
            more = min(most - holding[i], max(1, left * weights[i] // mass), surplus)
            holding[i] = holding[i] + more
            surplus = surplus - more
    return np.array([most] + holding)


def uneven(key, amount, total, most, lean):
    if amount == 2:
        one = jax.random.randint(key, (), max(1, total - most), min(most, total - 1) + 1)
        return jnp.stack([one, total - one])
    tallies = jnp.asarray(profile(amount, total, most, lean), jnp.int32)
    couples = (amount - 1) // 2
    giver, taker = tallies[1:1 + 2 * couples:2], tallies[2:2 + 2 * couples:2]
    room = jnp.minimum(giver - 1, most - taker)
    moved = jax.random.randint(jax.random.fold_in(key, 1), (couples,), 0, 1 << 20) % (room + 1)
    tallies = tallies.at[1:1 + 2 * couples:2].set(giver - moved).at[2:2 + 2 * couples:2].set(taker + moved)
    return tallies[jax.random.permutation(jax.random.fold_in(key, 2), amount)]


def routed_block(key, own, number, rows, number_of, top, reach, skew):
    ranking = jax.random.permutation(key, number_of)
    heavy_load, usual = portions_of(number_of, rows * top, reach, skew, True), portions_of(number_of, rows * top, reach, skew, False)
    places = jnp.arange(number_of)

    def named(sizes, rotation):
        used = int((sizes > 0).sum())
        fixed = max(1, used // 4)
        passed = fixed + (places - fixed + rotation * (used - fixed)) % max(1, number_of - fixed)
        return jnp.zeros((number_of,), jnp.int32).at[ranking[jnp.where(places < fixed, places, passed)]].set(jnp.asarray(sizes, jnp.int32))

    sizes = jnp.where(number % 4 == 0, named(heavy_load, number // 4), named(usual, number - number // 4 - 1))
    mixed = jax.random.permutation(jax.random.fold_in(own, 3), number_of)
    giver, taker = mixed[0:number_of // 2 * 2:2], mixed[1:number_of // 2 * 2:2]
    room = jnp.minimum(sizes[giver] - 1, reach - sizes[taker]) // 2
    room = jnp.where((giver == ranking[0]) | (taker == ranking[0]) | (sizes[taker] == 0), 0, jnp.maximum(room, 0))
    passed = jax.random.randint(jax.random.fold_in(own, 4), (number_of // 2,), 0, 1 << 20) % (room + 1)
    sizes = sizes.at[giver].add(-passed).at[taker].add(passed)
    labels = jnp.searchsorted(jnp.cumsum(sizes), jnp.arange(rows * top), side="right").astype(jnp.int32)
    table = labels.reshape(top, rows).T
    table = table[jax.random.permutation(jax.random.fold_in(own, 1), rows)]
    rotation = jax.random.randint(jax.random.fold_in(own, 2), (rows, 1), 0, top)
    return jnp.take_along_axis(table, (jnp.arange(top)[None, :] + rotation) % top, axis=1)


def portions_of(amount, total, most, slope, full):
    weights = [(1 << 20) // math.isqrt(rank ** slope) + 1 for rank in range(1, amount + 1)]
    largest = most if full else min(most, max(-(-total // amount), total * weights[0] // sum(weights)))
    least = 1 if total - largest >= amount - 1 else 0
    given, rest = [largest] + [least] * (amount - 1), total - largest - least * (amount - 1)
    while rest > 0:
        movable = [i for i in range(1, amount) if given[i] < largest] or [i for i in range(1, amount) if given[i] < most]
        whole, left = sum([weights[i] for i in movable]), rest
        for i in movable:
            more = min(most - given[i], max(1, left * weights[i] // whole), rest)
            given[i] = given[i] + more
            rest = rest - more
    return np.array(given)


def centred(stream_key, extent, scale, bound, pieces=(), held_as=jnp.bfloat16):
    values = scale * jax.random.normal(stream_key, extent, jnp.float32)
    if pieces:
        values = values * block_scale(stream_key, extent, pieces, -0.22, 0.18)
    return jnp.clip(values, -bound, bound).astype(held_as)


def setup_inputs(seed: int = 0) -> dict:
    arg_keys = jax.random.split(jax.random.key(seed), 9)
    coef = centred(arg_keys[0], (M, NN, 2 * FIELDS * LEV), 1.0, 6.0, ((0, 512),))
    leg = centred(arg_keys[1], (M, NLAT, NN), NN ** -0.5, 0.15625, ((0, 512),))
    vcoef = centred(arg_keys[2], (FIELDS, BAND, LEV), 0.4, 2.4, ((0, 4),), jnp.float32)
    obs_value = centred(arg_keys[3], (FIELDS, LEV, OBS_TOTAL), 1.0, 6.0, ((0, 4), (2, 128)))
    obs_weight = jnp.clip(jnp.exp(math.log(10.0) - 2.3025851 * jax.random.uniform(arg_keys[4], (FIELDS, LEV, OBS_TOTAL), jnp.float32) ** block_scale(arg_keys[4], (FIELDS, LEV, OBS_TOTAL), ((0, 4), (2, 128)), -0.2, 0.2)), 1.0, 10.0)
    obs_dest_keys = jax.random.split(jax.random.fold_in(arg_keys[5], 1), OBS_TOTAL // OBS_DEV)
    obs_dest_turns = jax.random.permutation(jax.random.fold_in(arg_keys[5], 3), OBS_TOTAL // OBS_DEV)
    obs_dest = jax.vmap(lambda own, number: routed_block(jax.random.fold_in(arg_keys[5], 2), own, number, OBS_DEV, N_BLK, 1, CAP, 2))(obs_dest_keys, obs_dest_turns).reshape((OBS_TOTAL, 1))
    obs_spot = plant(jax.random.randint(arg_keys[6], (OBS_TOTAL,), 0, LAT_DEV * NLON), jax.random.fold_in(arg_keys[6], 1), 0, (LAT_DEV * NLON) - 1).astype(jnp.int32)
    obs_count = uneven(arg_keys[7], N_BLK, (3 * N_BLK + 1) * OBS_DEV // 4, OBS_DEV, 2).astype(jnp.int32)
    return {"coef": coef, "leg": leg, "vcoef": vcoef, "obs_value": obs_value, "obs_weight": obs_weight, "obs_dest": obs_dest, "obs_spot": obs_spot, "obs_count": obs_count}


def zonal_table(start, count, waves, nlon):
    wave_ids = jnp.arange(waves, dtype=jnp.int32)
    longitude = start + jnp.arange(count, dtype=jnp.int32)
    phase = wave_ids[:, None] * longitude[None, :] % nlon
    angle = phase.astype(jnp.float32) * (2.0 * math.pi / nlon)
    both = jnp.stack([jnp.cos(angle), jnp.sin(angle)], axis=1)
    return both.reshape(2 * waves, count).astype(jnp.bfloat16)

def vertical(grid, coefs):
    padded = jnp.pad(grid, ((0, 0), (0, 0), (HALF, HALF), (0, 0)))
    total = jnp.zeros(grid.shape, jnp.float32)
    for shift in range(2 * HALF + 1):
        total = total + coefs[:, None, shift, :, None] * padded[:, :, shift:shift + LEV, :]
    return total

def vertical_adjoint(field, coefs):
    total = jnp.zeros(field.shape, jnp.float32)
    for shift in range(2 * HALF + 1):
        term = coefs[:, None, shift, :, None] * field
        padded = jnp.pad(term, ((0, 0), (0, 0), (HALF, HALF), (0, 0)))
        begin = 2 * HALF - shift
        total = total + padded[:, :, begin:begin + LEV, :]
    return total

def reference(coef, leg, vcoef, obs_value, obs_weight, obs_dest, obs_spot, obs_count):
    width = 2 * FIELDS * LEV

    def legendre(pair):
        return jnp.dot(pair[0], pair[1], preferred_element_type=jnp.float32).astype(jnp.bfloat16)
    four = lax.map(legendre, (leg, coef)).reshape(M, NLAT, 2, FIELDS, LEV)
    rows = jnp.transpose(four, (3, 1, 4, 0, 2)).reshape(FIELDS * NLAT * LEV, 2 * M)
    table = zonal_table(0, NLON, M, NLON)
    scale = 1.0 / math.sqrt(M)
    grid = (jnp.dot(rows, table, preferred_element_type=jnp.float32) * scale).reshape(FIELDS, NLAT, LEV, NLON)
    incr = vertical(grid, vcoef)
    dest = obs_dest[:, 0]
    index = jnp.arange(OBS_TOTAL, dtype=jnp.int32)
    live = (index % OBS_DEV < obs_count[index // OBS_DEV]).astype(jnp.float32)
    latitude = dest * LAT_DEV + obs_spot // NLON
    longitude = obs_spot % NLON
    model = jnp.transpose(incr[:, latitude, :, longitude], (1, 2, 0))
    weighted = obs_weight * (model - obs_value.astype(jnp.float32)) * live[None, None, :]
    adjoint = jnp.zeros((FIELDS, NLAT, LEV, NLON), jnp.float32)
    adjoint = adjoint.at[:, latitude, :, longitude].add(jnp.transpose(weighted, (2, 0, 1)))
    back = vertical_adjoint(adjoint, vcoef).astype(jnp.bfloat16)
    spectral = jnp.dot(back.reshape(FIELDS * NLAT * LEV, NLON), table.T, preferred_element_type=jnp.float32)
    wave = (spectral * scale).astype(jnp.bfloat16).reshape(FIELDS, NLAT, LEV, M, 2)
    wave = jnp.transpose(wave, (3, 1, 4, 0, 2)).reshape(M, NLAT, width)

    def legendre_adjoint(pair):
        return jnp.dot(pair[0].T, pair[1], preferred_element_type=jnp.float32).astype(jnp.bfloat16)
    return lax.map(legendre_adjoint, (leg, wave))
```

```python
import functools
import math

import jax
import jax.numpy as jnp
import numpy as np
from jax import lax
from jax.experimental import pallas as pl
from jax.experimental.pallas import tpu as pltpu
from jax.sharding import PartitionSpec as P

NLON = 2560
NY = 4
SLOT_ROWS = 4
MESH = pl.DeviceIdType.MESH
F32 = jnp.float32
BF16 = jnp.bfloat16


def power_series(f, terms):
    fit = np.polynomial.chebyshev.Chebyshev.interpolate(f, terms - 1, domain=[0.0, 0.25])
    return [float(c) for c in fit.convert(kind=np.polynomial.Polynomial).coef]


def cos_series():
    return power_series(lambda v: np.cos(2 * np.pi * np.sqrt(v)), 7)


def sin_series():
    return power_series(lambda v: 2 * np.pi * np.sinc(2 * np.sqrt(v)), 7)


def horner(coefs, v):
    total = jnp.full_like(v, coefs[-1])
    for c in coefs[-2::-1]:
        total = total * v + c
    return total


def cos_sin(turns, whole):
    rest = turns - jnp.round(turns * (1.0 / whole)) * whole
    u = rest * (1.0 / whole)
    v = u * u
    return horner(cos_series(), v), u * horner(sin_series(), v)


def dot(a, b, dims=(1, 0), precision=None):
    return lax.dot_general(
        a, b, (((dims[0],), (dims[1],)), ((), ())), precision=precision, preferred_element_type=F32
    )


def iota(shape, axis):
    return lax.broadcasted_iota(jnp.int32, shape, axis)


def kernel(
    nblk, nfld, ny, leg_hbm, coef_hbm, vcoef_ref, val_ref, wgt_ref, dest_ref, spot_ref, count_ref, wave_ref,
    leg, coef, rows_f, tmp_a, tmp_o, tmp_p, send_a, recv_a, send_b, recv_b, send_oa, recv_oa, send_ob, recv_ob,
    send_c, recv_c, send_d, recv_d, spot_col, spot_row, tcos, tsin, ucos, usin,
    load_sem, sa_s, sa_r, sb_s, sb_r, oa_s, oa_r, ob_s, ob_r, sc_s, sc_r, sd_s, sd_r,
):
    nxz = nblk // ny
    nz = nxz // 2
    group = ny * nfld
    waves, lat = leg.shape[0], leg.shape[1]
    members = group * waves
    total_m = nxz * members
    levels = vcoef_ref.shape[1]
    band = vcoef_ref.shape[0]
    half = (band - 1) // 2
    lanes = 4 * levels
    obs_dev = dest_ref.shape[1]
    orows = nblk * SLOT_ROWS

    b = lax.axis_index("blk")
    f = lax.axis_index("fld")
    y = lax.rem(b, ny)
    xz = lax.div(b, ny)
    member = y * nfld + f

    def xz_partner(i):
        flip = lax.rem(i, 2)
        t = lax.div(i, 2)
        step = lax.div(t + 1, 2)
        move = jnp.where(lax.rem(t, 2) == 1, step, nz - step)
        x_hi = lax.rem(lax.div(xz, nz) + flip, 2)
        z = lax.rem(lax.rem(xz, nz) + move, nz)
        return x_hi * nz + z

    def group_partner(i):
        return lax.rem(member + i, group)

    def y_partner(i):
        return lax.rem(y + i, ny)

    def group_device(mem):
        return (xz * ny + lax.div(mem, nfld), lax.rem(mem, nfld))

    def xz_device(other):
        return (other * ny + y, f)

    def y_device(other):
        return (xz * ny + other, f)

    def copy_of(src, dst, where_from, where_to, send_sem, recv_sem, device):
        return pltpu.make_async_remote_copy(
            src_ref=src.at[where_from], dst_ref=dst.at[where_to], send_sem=send_sem.at[where_from],
            recv_sem=recv_sem.at[where_to], device_id=device, device_id_type=MESH,
        )

    def start_all(count, partner, device, src, dst, mine, send_sem, recv_sem):
        def step(k, carry):
            other = partner(count - 1 - k)
            copy_of(src, dst, other, mine, send_sem, recv_sem, device(other)).start()
            return carry

        lax.fori_loop(0, count - 1, step, 0)
        dst[mine] = src[mine]

    def recv_all(count, partner, device, src, dst, send_sem, recv_sem):
        def step(k, carry):
            other = partner(count - 1 - k)
            copy_of(src, dst, other, other, send_sem, recv_sem, device(other)).wait_recv()
            return carry

        lax.fori_loop(0, count - 1, step, 0)

    def send_done(count, partner, device, src, dst, send_sem, recv_sem):
        def step(k, carry):
            other = partner(count - 1 - k)
            copy_of(src, dst, other, other, send_sem, recv_sem, device(other)).wait_send()
            return carry

        lax.fori_loop(0, count - 1, step, 0)

    in_group = (group, group_partner, group_device)
    in_xz = (nxz, xz_partner, xz_device)
    in_y = (ny, y_partner, y_device)

    load_leg = pltpu.make_async_copy(leg_hbm, leg, load_sem.at[0])
    load_coef = pltpu.make_async_copy(coef_hbm, coef, load_sem.at[1])
    load_coef.start()
    load_leg.start()
    barrier = pltpu.get_barrier_semaphore()

    def greet(count, partner, device):
        def step(i, carry):
            pl.semaphore_signal(barrier, inc=1, device_id=device(partner(i)), device_id_type=MESH)
            return carry

        lax.fori_loop(1, count, step, 0)

    greet(*in_group)
    greet(*in_xz)

    dest = dest_ref[...]
    spot = spot_ref[...]
    order = iota((1, obs_dev), 1)
    live = order < count_ref[0]
    onehot = (iota((nblk, obs_dev), 0) == dest).astype(F32)
    earlier = (iota((obs_dev, obs_dev), 0) < iota((obs_dev, obs_dev), 1)).astype(BF16)
    before = dot(onehot.astype(BF16), earlier)
    rank = jnp.sum(before * onehot, axis=0, keepdims=True).astype(jnp.int32)
    place = (lax.rem(dest, ny) * nxz + lax.div(dest, ny)) * SLOT_ROWS
    place = jnp.where(live, place, -SLOT_ROWS)
    pair = place + lax.div(rank, 2)
    second = lax.rem(rank, 2) == 1
    row = iota((orows, obs_dev), 0)
    pick_first = (row == jnp.where(second, -1, pair)).astype(BF16)
    pick_second = (row == jnp.where(second, pair, -1)).astype(BF16)
    pick_place = (row == place + SLOT_ROWS - 1).astype(BF16)
    data = jnp.concatenate([val_ref[...].astype(F32), wgt_ref[...]], axis=0).astype(BF16)
    lane_q = iota((lanes // 2, obs_dev), 0)
    high = lax.div(spot, 32)
    low = spot - high * 32
    spots = jnp.where(lane_q == rank, high, jnp.where(lane_q == rank + 8, low, 0)).astype(F32).astype(BF16)
    none = jnp.zeros((lanes // 2, obs_dev), BF16)
    packed = dot(pick_first, jnp.concatenate([data, none], axis=0), (1, 1))
    packed = packed + dot(pick_second, jnp.concatenate([none, data], axis=0), (1, 1))
    packed = packed + dot(pick_place, jnp.concatenate([spots, none], axis=0), (1, 1))
    send_oa[...] = packed.astype(BF16).reshape(send_oa.shape)

    def greet_wait():
        pl.semaphore_wait(barrier, group - 1 + nxz - 1)

    load_coef.wait()
    load_leg.wait()
    for w in range(waves):
        result = dot(leg[w], coef[w])
        for r in range(2):
            rows_f[pl.ds((r * waves + w) * lat, lat), :] = result[:, r * lanes : (r + 1) * lanes]
    greet_wait()
    start_all(*in_y, send_oa, recv_oa, y, oa_s, oa_r)

    chunk = lax.div(iota((nxz, lanes), 1), levels)

    def pack(step, carry):
        w, yy = lax.div(step, ny), lax.rem(step, ny)
        parts = []
        for r in range(2):
            for j in range(2):
                parts.append(rows_f[pl.ds((r * waves + w) * lat + 2 * yy + j, nxz, stride=2 * ny), :])
        for ff in range(nfld):
            out = parts[0] if ff == 0 else pltpu.roll(parts[0], (0 - ff) % 4 * levels, 1)
            for k in range(1, 4):
                moved = parts[k] if ff == k else pltpu.roll(parts[k], (k - ff) % 4 * levels, 1)
                out = jnp.where(chunk == k, moved, out)
            send_a[yy * nfld + ff, pl.ds(pl.multiple_of(w * nxz, nxz), nxz), :] = out.astype(BF16)
        return carry

    lax.fori_loop(0, waves * ny, pack, 0)
    start_all(*in_group, send_a, recv_a, member, sa_s, sa_r)

    recv_all(*in_y, send_oa, recv_oa, oa_s, oa_r)
    tmp_o[...] = recv_oa[...].astype(F32).reshape(tmp_o.shape)
    for yy in range(ny):
        for k in range(SLOT_ROWS):
            rows = tmp_o[pl.ds(yy * nxz * SLOT_ROWS + k, nxz, stride=SLOT_ROWS), :]
            tmp_p[pl.ds(yy * SLOT_ROWS + k, nxz, stride=ny * SLOT_ROWS), :] = rows
    send_ob[...] = tmp_p[...].astype(BF16).reshape(send_ob.shape)
    start_all(*in_xz, send_ob, recv_ob, xz, ob_s, ob_r)

    def swap(src, dst, outer, inner):
        tmp_a[...] = src[...].astype(F32).reshape(tmp_a.shape)
        for i in range(inner):
            rows = tmp_a[pl.ds(i, outer, stride=inner), :]
            per = dst.shape[1] // outer
            dst[i // per, pl.ds(i % per * outer, outer), :] = rows.astype(BF16)

    recv_all(*in_group, send_a, recv_a, sa_s, sa_r)
    swap(recv_a, send_b, members, nxz)
    start_all(*in_xz, send_b, recv_b, xz, sb_s, sb_r)

    recv_all(*in_xz, send_ob, recv_ob, ob_s, ob_r)
    got = recv_ob[...].reshape(orows, lanes)
    in_row = lax.rem(iota((orows, orows), 0), SLOT_ROWS)
    places = iota((orows, orows), 0) - in_row + (SLOT_ROWS - 1)
    spread = dot((iota((orows, orows), 1) == places).astype(BF16), got)
    lane = iota((orows, lanes), 1)
    k_row = lax.rem(iota((orows, lanes), 0), SLOT_ROWS)
    ones = jnp.ones((lanes, lanes), BF16)
    base = min(lanes, total_m)
    for h in range(2):
        q = 2 * k_row + h
        mine = jnp.where(lane == q, spread * 32.0, jnp.where(lane == q + 8, spread, 0.0)).astype(BF16)
        spot_col[h] = dot(mine, ones)
        spot_row[h] = dot(ones, mine, (1, 1))

    def longitude(s):
        return jnp.where(s >= NLON, s - NLON, s)

    def turn(c, s, c1, s1):
        return c * c1 - s * s1, s * c1 + c * s1

    tile = min(64, orows)
    for h in range(2):
        def along_m(i, carry):
            here = pl.ds(pl.multiple_of(i * tile, tile), tile)
            lon = longitude(spot_col[h, here, pl.ds(0, base)])
            c, s = cos_sin(lon * iota((tile, base), 1).astype(F32), NLON)
            c1, s1 = cos_sin(lon * float(base), NLON)
            for q in range(total_m // base):
                tcos[h, here, pl.ds(q * base, base)] = c.astype(BF16)
                tsin[h, here, pl.ds(q * base, base)] = s.astype(BF16)
                c, s = turn(c, s, c1, s1)
            return carry

        lax.fori_loop(0, orows // tile, along_m, 0)

    deep = min(64, total_m)
    wide = min(128, orows)
    for h in range(2):
        def along_o(i, carry):
            here = pl.ds(pl.multiple_of(i * wide, wide), wide)
            lon = longitude(spot_row[h, pl.ds(0, deep), here])
            c, s = cos_sin(lon * iota((deep, wide), 0).astype(F32), NLON)
            c1, s1 = cos_sin(lon * float(deep), NLON)
            for q in range(total_m // deep):
                ucos[h, pl.ds(q * deep, deep), here] = c.astype(BF16)
                usin[h, pl.ds(q * deep, deep), here] = s.astype(BF16)
                c, s = turn(c, s, c1, s1)
            return carry

        lax.fori_loop(0, orows // wide, along_o, 0)

    scale = 1.0 / math.sqrt(total_m)
    vc = jnp.concatenate([vcoef_ref[...]] * 4, axis=1) * scale
    lev_row = lax.rem(iota((lanes, lanes), 0), levels)
    lev_col = lax.rem(iota((lanes, lanes), 1), levels)
    up = jnp.zeros((lanes, lanes), F32)
    for k in range(band):
        up = up + jnp.where(lev_row == lev_col + (k - half), vc[k : k + 1, :], 0.0)
    ups, downs = [], []
    for h in range(2):
        in_half = lax.div(iota((lanes, lanes), 1), levels) == 2 * h
        first = lax.div(iota((lanes, lanes), 0), levels) < 2
        ups.append(jnp.where(in_half & first, up, 0.0))
        downs.append(jnp.where(in_half, up, 0.0))
    exact = lax.Precision.HIGHEST
    chunk_o = lax.div(lane, levels)
    got32 = got.astype(F32)
    weight = pltpu.roll(got32, lanes - levels, 1)
    weight = jnp.where(lax.rem(chunk_o, 2) == 0, weight, 0.0)

    recv_all(*in_xz, send_b, recv_b, sb_s, sb_r)
    four = recv_b[...].reshape(total_m, lanes)
    model = jnp.zeros((orows, lanes), F32)
    at_lat = []
    for h in range(2):
        at_lat.append(lax.rem(chunk_o, 2) == (spot_col[h] >= NLON).astype(jnp.int32))
        grid = dot(tcos[h], four) + pltpu.roll(dot(tsin[h], four), lanes // 2, 1)
        grid = jnp.where(at_lat[h] & (chunk_o < 2), grid, 0.0)
        model = model + dot(grid, ups[h], precision=exact)
    weighted = weight * (model - got32)
    wave = jnp.zeros((total_m, lanes), F32)
    for h in range(2):
        back = dot(weighted, downs[h], (1, 1), precision=exact)
        back = jnp.where(at_lat[h], back, 0.0)
        wave = wave + dot(ucos[h], jnp.where(chunk_o < 2, back, 0.0).astype(BF16))
        wave = wave + dot(usin[h], jnp.where(chunk_o < 2, 0.0, back).astype(BF16))
    send_c[...] = wave.astype(BF16).reshape(send_c.shape)
    start_all(*in_xz, send_c, recv_c, xz, sc_s, sc_r)
    recv_all(*in_xz, send_c, recv_c, sc_s, sc_r)
    swap(recv_c, send_d, nxz, members)
    start_all(*in_group, send_d, recv_d, member, sd_s, sd_r)
    recv_all(*in_group, send_d, recv_d, sd_s, sd_r)

    def unpack(step, carry):
        w, yy = lax.div(step, ny), lax.rem(step, ny)
        parts = [
            recv_d[yy * nfld + ff, pl.ds(pl.multiple_of(w * nxz, nxz), nxz), :].astype(F32)
            for ff in range(nfld)
        ]
        for r in range(2):
            for j in range(2):
                k = 2 * r + j
                out = parts[0] if k == 0 else pltpu.roll(parts[0], (0 - k) % 4 * levels, 1)
                for ff in range(1, nfld):
                    moved = parts[ff] if ff == k else pltpu.roll(parts[ff], (ff - k) % 4 * levels, 1)
                    out = jnp.where(chunk == ff, moved, out)
                rows_f[pl.ds((r * waves + w) * lat + 2 * yy + j, nxz, stride=2 * ny), :] = out
        return carry

    lax.fori_loop(0, waves * ny, unpack, 0)
    for w in range(waves):
        for r in range(2):
            rows = rows_f[pl.ds((r * waves + w) * lat, lat), :]
            wave_ref[w, :, pl.ds(r * lanes, lanes)] = rows.astype(BF16)

    for sent in (
        (*in_y, send_oa, recv_oa, oa_s, oa_r),
        (*in_group, send_a, recv_a, sa_s, sa_r),
        (*in_xz, send_ob, recv_ob, ob_s, ob_r),
        (*in_xz, send_b, recv_b, sb_s, sb_r),
        (*in_xz, send_c, recv_c, sc_s, sc_r),
        (*in_group, send_d, recv_d, sd_s, sd_r),
    ):
        send_done(*sent)


def on_device(coef, leg, vcoef, obs_value, obs_weight, obs_dest, obs_spot, obs_count, ny=NY):
    nblk = lax.axis_size("blk")
    nfld = lax.axis_size("fld")
    waves, lat, nn = leg.shape
    width = coef.shape[2]
    levels = vcoef.shape[2]
    lanes = 4 * levels
    nxz = nblk // ny
    group = ny * nfld
    members = group * waves
    total_m = nxz * members
    orows = nblk * SLOT_ROWS
    obs_dev = obs_spot.shape[0]

    def buffer(*shape):
        return pltpu.VMEM(shape, BF16)

    vmem = pl.BlockSpec(memory_space=pltpu.VMEM)
    scratch = [
        buffer(waves, lat, nn), buffer(waves, nn, width), pltpu.VMEM((2 * waves * lat, lanes), F32),
        pltpu.VMEM((total_m, lanes), F32), pltpu.VMEM((orows, lanes), F32), pltpu.VMEM((orows, lanes), F32),
        buffer(group, waves * nxz, lanes), buffer(group, waves * nxz, lanes),
        buffer(nxz, members, lanes), buffer(nxz, members, lanes),
        buffer(ny, nxz * SLOT_ROWS, lanes), buffer(ny, nxz * SLOT_ROWS, lanes),
        buffer(nxz, ny * SLOT_ROWS, lanes), buffer(nxz, ny * SLOT_ROWS, lanes),
        buffer(nxz, members, lanes), buffer(nxz, members, lanes),
        buffer(group, waves * nxz, lanes), buffer(group, waves * nxz, lanes),
        pltpu.VMEM((2, orows, lanes), F32), pltpu.VMEM((2, lanes, orows), F32),
        buffer(2, orows, total_m), buffer(2, orows, total_m),
        buffer(2, total_m, orows), buffer(2, total_m, orows),
        pltpu.SemaphoreType.DMA((2,)),
    ]
    for count in (group, nxz, ny, nxz, nxz, group):
        scratch += [pltpu.SemaphoreType.DMA((count,)), pltpu.SemaphoreType.DMA((count,))]
    wave = pl.pallas_call(
        functools.partial(kernel, nblk, nfld, ny),
        out_shape=jax.ShapeDtypeStruct((waves, lat, width), BF16),
        in_specs=[
            pl.BlockSpec(memory_space=pl.ANY), pl.BlockSpec(memory_space=pl.ANY), vmem, vmem, vmem, vmem, vmem,
            pl.BlockSpec(memory_space=pltpu.SMEM),
        ],
        out_specs=vmem,
        scratch_shapes=scratch,
        compiler_params=pltpu.CompilerParams(
            collective_id=0, has_side_effects=True, vmem_limit_bytes=48 * 1024 * 1024
        ),
    )(leg, coef, vcoef[0], obs_value[0], obs_weight[0], obs_dest.reshape(1, obs_dev), obs_spot.reshape(1, obs_dev), obs_count)
    return jnp.einsum("mjn,mjc->mnc", leg, wave, preferred_element_type=F32).astype(BF16)


def solution(mesh):
    in_specs = (
        P(("blk", "fld"), None, None),
        P(("blk", "fld"), None, None),
        P("fld", None, None),
        P("fld", None, "blk"),
        P("fld", None, "blk"),
        P("blk", None),
        P("blk"),
        P("blk"),
    )
    out_specs = P(("blk", "fld"), None, None)
    return jax.shard_map(
        on_device, mesh=mesh, in_specs=in_specs, out_specs=out_specs, check_vma=False
    )
```

```python
import functools
import math

import jax
import jax.numpy as jnp
import numpy as np
from jax import lax
from jax.experimental import pallas as pl
from jax.experimental.pallas import tpu as pltpu
from jax.sharding import PartitionSpec as P

NLON = 2560
NY = 4
SLOT_ROWS = 4
MESH = pl.DeviceIdType.MESH
F32 = jnp.float32
BF16 = jnp.bfloat16


def power_series(f, terms):
    fit = np.polynomial.chebyshev.Chebyshev.interpolate(f, terms - 1, domain=[0.0, 0.25])
    return [float(c) for c in fit.convert(kind=np.polynomial.Polynomial).coef]


def cos_series():
    return power_series(lambda v: np.cos(2 * np.pi * np.sqrt(v)), 7)


def sin_series():
    return power_series(lambda v: 2 * np.pi * np.sinc(2 * np.sqrt(v)), 7)


def horner(coefs, v):
    total = jnp.full_like(v, coefs[-1])
    for c in coefs[-2::-1]:
        total = total * v + c
    return total


def cos_sin(turns, whole):
    rest = turns - jnp.round(turns * (1.0 / whole)) * whole
    u = rest * (1.0 / whole)
    v = u * u
    return horner(cos_series(), v), u * horner(sin_series(), v)


def dot(a, b, dims=(1, 0), precision=None):
    return lax.dot_general(
        a, b, (((dims[0],), (dims[1],)), ((), ())), precision=precision, preferred_element_type=F32
    )


def iota(shape, axis):
    return lax.broadcasted_iota(jnp.int32, shape, axis)


def kernel(
    nblk, nfld, ny, leg_hbm, coef_hbm, vcoef_hbm, val_hbm, wgt_hbm, dest_hbm, spot_hbm, count_ref, wave_hbm, turned_hbm,
    wave_ref, turned_ref, leg, coef, vcoef_ref, val_ref, wgt_ref, dest_ref, spot_ref, rows_f, tmp_o, send_a, recv_a, send_b, recv_b, send_oa, recv_oa, send_ob, recv_ob,
    send_c, recv_c, send_d, recv_d, spot_col, spot_row, table, flipped,
    load_sem, store_sem, sa_s, sa_r, sb_s, sb_r, oa_s, oa_r, ob_s, ob_r, sc_s, sc_r, sd_s, sd_r,
):
    nxz = nblk // ny
    nz = nxz // 2
    group = ny * nfld
    waves, lat = leg.shape[0], leg.shape[1]
    part_m = nxz * group
    total_m = waves * part_m
    levels = vcoef_ref.shape[2]
    band = vcoef_ref.shape[0]
    half = (band - 1) // 2
    lanes = 4 * levels
    obs_dev = dest_ref.shape[1]
    orows = nblk * SLOT_ROWS

    b = lax.axis_index("blk")
    f = lax.axis_index("fld")
    y = lax.rem(b, ny)
    xz = lax.div(b, ny)
    member = y * nfld + f

    def xz_partner(i):
        flip = lax.rem(i, 2)
        t = lax.div(i, 2)
        step = lax.div(t + 1, 2)
        move = jnp.where(lax.rem(t, 2) == 1, step, nz - step)
        x_hi = lax.rem(lax.div(xz, nz) + flip, 2)
        z = lax.rem(lax.rem(xz, nz) + move, nz)
        return x_hi * nz + z

    def group_partner(i):
        return lax.rem(member + i, group)

    def y_partner(i):
        return lax.rem(y + i, ny)

    def group_device(mem):
        return (xz * ny + lax.div(mem, nfld), lax.rem(mem, nfld))

    def xz_device(other):
        return (other * ny + y, f)

    def y_device(other):
        return (xz * ny + other, f)

    def start_all(part, count, partner, device, mine, src, dst, send_sem, recv_sem):
        def step(k, carry):
            other = partner(count - 1 - k)
            pltpu.make_async_remote_copy(
                src_ref=src.at[part, other], dst_ref=dst.at[part, mine], send_sem=send_sem.at[part],
                recv_sem=recv_sem.at[part], device_id=device(other), device_id_type=MESH,
            ).start()
            return carry

        lax.fori_loop(0, count - 1, step, 0)
        dst[part, mine] = src[part, mine]

    def whole(part, count, partner, device, mine, src, dst, send_sem, recv_sem):
        others = pl.ds(0, count - 1)
        return pltpu.make_async_remote_copy(
            src_ref=src.at[part, others], dst_ref=dst.at[part, others], send_sem=send_sem.at[part],
            recv_sem=recv_sem.at[part], device_id=device(partner(1)), device_id_type=MESH,
        )

    def recv_all(part, *stage):
        whole(part, *stage).wait_recv()

    def send_done(part, *stage):
        whole(part, *stage).wait_send()

    in_group = (group, group_partner, group_device, member)
    in_xz = (nxz, xz_partner, xz_device, xz)
    in_y = (ny, y_partner, y_device, y)
    stage_a = (*in_group, send_a, recv_a, sa_s, sa_r)
    stage_b = (*in_xz, send_b, recv_b, sb_s, sb_r)
    stage_c = (*in_xz, send_c, recv_c, sc_s, sc_r)
    stage_d = (*in_group, send_d, recv_d, sd_s, sd_r)
    obs_xz = (*in_xz, send_ob, recv_ob, ob_s, ob_r)
    obs_y = (*in_y, send_oa, recv_oa, oa_s, oa_r)

    loads = [
        pltpu.make_async_copy(src, dst, load_sem.at[i])
        for i, (src, dst) in enumerate(
            (
                (dest_hbm, dest_ref), (spot_hbm, spot_ref), (val_hbm, val_ref), (wgt_hbm, wgt_ref),
                (vcoef_hbm, vcoef_ref), (coef_hbm, coef), (leg_hbm, leg),
            )
        )
    ]
    for load in loads:
        load.start()
    barrier = pltpu.get_barrier_semaphore()

    def greet(count, partner, device, mine):
        def step(i, carry):
            pl.semaphore_signal(barrier, inc=1, device_id=device(partner(i)), device_id_type=MESH)
            return carry

        lax.fori_loop(1, count, step, 0)

    greet(*in_group)
    greet(*in_xz)

    for load in loads[:5]:
        load.wait()

    dest = dest_ref[...]
    spot = spot_ref[...]
    live = iota((1, obs_dev), 1) < count_ref[0]
    place = jnp.where(live, lax.rem(dest, ny) * nxz + lax.div(dest, ny), -1)
    onehot = (iota((nblk, obs_dev), 0) == place).astype(BF16)
    part = min(128, obs_dev)
    upto = iota((part, 2 * part), 0) < iota((part, 2 * part), 1)
    ranks = []
    carry = jnp.zeros((nblk, part), F32)
    for i in range(obs_dev // part):
        piece = onehot[:, i * part : (i + 1) * part]
        counted = dot(piece, upto.astype(BF16))
        ranks.append(jnp.sum((counted[:, :part] + carry) * piece.astype(F32), axis=0, keepdims=True))
        carry = carry + counted[:, part:]
    rank = jnp.concatenate(ranks, axis=1).astype(jnp.int32)
    data = jnp.concatenate([val_ref[...].astype(F32), wgt_ref[...]], axis=0)
    lane_q = iota((lanes, obs_dev), 0)
    high = lax.div(spot, 32)
    low = spot - high * 32
    spots = jnp.where(lane_q == rank, high, jnp.where(lane_q == rank + 8, low, 0)).astype(F32)
    for k in range(SLOT_ROWS):
        rows = spots
        if k < SLOT_ROWS - 1:
            rows = [jnp.where(rank == 2 * k + h, data, 0.0) for h in range(2)]
            rows = jnp.concatenate(rows, axis=0)
        packed = dot(onehot, rows.astype(BF16), (1, 1))
        for yy in range(ny):
            tmp_o[pl.ds(yy * SLOT_ROWS + k, nxz, stride=ny * SLOT_ROWS), :] = packed[yy * nxz : (yy + 1) * nxz]
    send_ob[...] = tmp_o[...].astype(BF16).reshape(send_ob.shape)

    chunk = lax.div(iota((nxz, lanes), 1), levels)

    def legendre(w):
        result = dot(leg[w], coef[w])
        for r in range(2):
            rows_f[pl.ds((r * waves + w) * lat, lat), :] = result[:, r * lanes : (r + 1) * lanes]
        for yy in range(ny):
            parts = [
                rows_f[pl.ds((r * waves + w) * lat + 2 * yy + j, nxz, stride=2 * ny), :]
                for r in range(2)
                for j in range(2)
            ]
            for ff in range(nfld):
                out = parts[0] if ff == 0 else pltpu.roll(parts[0], (0 - ff) % 4 * levels, 1)
                for k in range(1, 4):
                    moved = parts[k] if ff == k else pltpu.roll(parts[k], (k - ff) % 4 * levels, 1)
                    out = jnp.where(chunk == k, moved, out)
                send_a[w, yy * nfld + ff] = out.astype(BF16)

    def swap(part, src, dst, outer, inner):
        tmp_o[...] = src[part].astype(F32).reshape(tmp_o.shape)
        per = dst.shape[2] // outer
        for i in range(inner):
            rows = tmp_o[pl.ds(i, outer, stride=inner), :]
            dst[part, i // per, pl.ds(i % per * outer, outer), :] = rows.astype(BF16)

    for load in loads[5:]:
        load.wait()
    legendre(0)
    pl.semaphore_wait(barrier, group - 1 + nxz - 1)
    start_all(0, *stage_a)
    start_all(0, *obs_xz)
    for w in range(1, waves):
        legendre(w)
        start_all(w, *stage_a)

    for w in range(waves):
        recv_all(w, *stage_a)
        swap(w, recv_a, send_b, group, nxz)
        start_all(w, *stage_b)

    recv_all(0, *obs_xz)
    swap(0, recv_ob, send_oa, nxz, ny * SLOT_ROWS)
    start_all(0, *obs_y)
    recv_all(0, *obs_y)

    got = recv_oa[...].reshape(orows, lanes)
    spread = [recv_oa[0, yy, pl.ds((SLOT_ROWS - 1) * nxz, nxz), :] for yy in range(ny) for k in range(SLOT_ROWS)]
    spread = jnp.concatenate(spread, axis=0).astype(F32)
    lane = iota((orows, lanes), 1)
    k_row = lax.rem(lax.div(iota((orows, lanes), 0), nxz), SLOT_ROWS)
    ones = jnp.ones((lanes, lanes), BF16)
    for h in range(2):
        q = 2 * k_row + h
        mine = jnp.where(lane == q, spread * 32.0, jnp.where(lane == q + 8, spread, 0.0)).astype(BF16)
        spot_col[h] = dot(mine, ones)
        spot_row[h] = dot(ones, mine, (1, 1))

    def longitude(s):
        return jnp.where(s >= NLON, s - NLON, s)

    def turn(c, s, c1, s1):
        return c * c1 - s * s1, s * c1 + c * s1

    tile = min(64, orows)
    base = min(lanes, part_m)
    for h in range(2):
        def along_m(i, carry):
            here = pl.ds(pl.multiple_of(i * tile, tile), tile)
            lon = longitude(spot_col[h, here, pl.ds(0, base)])
            c, s = cos_sin(lon * (waves * iota((tile, base), 1)).astype(F32), NLON)
            by_one = cos_sin(lon, NLON)
            by_base = cos_sin(lon * float(waves * base), NLON)
            for w in range(waves):
                if w > 0:
                    c, s = turn(*first, *by_one)
                first = (c, s)
                for q in range(part_m // base):
                    table[h, here, pl.ds(2 * w * part_m + q * base, base)] = c.astype(BF16)
                    table[h, here, pl.ds((2 * w + 1) * part_m + q * base, base)] = s.astype(BF16)
                    c, s = turn(c, s, *by_base)
            return carry

        lax.fori_loop(0, orows // tile, along_m, 0)

    deep = min(64, part_m)
    wide = min(128, orows)
    for h in range(2):
        def along_o(i, carry):
            here = pl.ds(pl.multiple_of(i * wide, wide), wide)
            there = [pl.ds(pl.multiple_of((2 * h + k) * orows + i * wide, wide), wide) for k in range(2)]
            lon = longitude(spot_row[h, pl.ds(0, deep), here])
            c, s = cos_sin(lon * (waves * iota((deep, wide), 0)).astype(F32), NLON)
            by_one = cos_sin(lon, NLON)
            by_deep = cos_sin(lon * float(waves * deep), NLON)
            for w in range(waves):
                if w > 0:
                    c, s = turn(*first, *by_one)
                first = (c, s)
                for q in range(part_m // deep):
                    flipped[pl.ds(w * part_m + q * deep, deep), there[0]] = c.astype(BF16)
                    flipped[pl.ds(w * part_m + q * deep, deep), there[1]] = s.astype(BF16)
                    c, s = turn(c, s, *by_deep)
            return carry

        lax.fori_loop(0, orows // wide, along_o, 0)

    scale = 1.0 / math.sqrt(total_m)
    vc = jnp.concatenate([vcoef_ref[:, 0, :]] * 4, axis=1) * scale
    lev_row = lax.rem(iota((lanes, lanes), 0), levels)
    lev_col = lax.rem(iota((lanes, lanes), 1), levels)
    up = jnp.zeros((lanes, lanes), F32)
    for k in range(band):
        up = up + jnp.where(lev_row == lev_col + (k - half), vc[k : k + 1, :], 0.0)
    col_chunk = lax.div(iota((lanes, lanes), 1), levels)
    row_chunk = lax.div(iota((lanes, lanes), 0), levels)
    ups = jnp.where(lax.div(row_chunk, 2) * 2 == col_chunk, up, 0.0)
    downs = jnp.concatenate([jnp.where(col_chunk == 2 * h, up, 0.0) for h in range(2)], axis=0)
    chunk_o = lax.div(lane, levels)
    got32 = got.astype(F32)
    weight = pltpu.roll(got32, lanes - levels, 1)
    weight = jnp.where(lax.rem(chunk_o, 2) == 0, weight, 0.0)

    def split(x):
        coarse = x.astype(BF16)
        return coarse, (x - coarse.astype(F32)).astype(BF16)

    def dot3(a, split_b, dims):
        a0, a1 = split(a)
        b0, b1 = split_b
        return dot(a0, b0, dims) + (dot(a1, b0, dims) + dot(a0, b1, dims))

    ups, downs = split(ups), split(downs)
    at_lat = [lax.rem(chunk_o, 2) == (spot_col[h] >= NLON).astype(jnp.int32) for h in range(2)]

    grids = [jnp.zeros((orows, lanes), F32) for h in range(2)]
    for w in range(waves):
        recv_all(w, *stage_b)
        four = recv_b[w].reshape(part_m, lanes)
        crossed = pltpu.roll(four.astype(F32), lanes // 2, 1).astype(BF16)
        sides = (jnp.concatenate([four, crossed], axis=0), jnp.concatenate([crossed, four], axis=0))
        for h in range(2):
            grids[h] = grids[h] + dot(table[h, :, pl.ds(2 * w * part_m, 2 * part_m)], sides[h])
    grids = [jnp.where(at_lat[h], grids[h], 0.0) for h in range(2)]
    grid = jnp.where(chunk_o < 2, grids[0], grids[1])
    weighted = weight * (dot3(grid, ups, (1, 0)) - got32)
    backs = dot3(weighted, downs, (1, 1))
    columns = []
    for h in range(2):
        back = jnp.where(at_lat[h], backs[:, h * lanes : (h + 1) * lanes], 0.0)
        columns += [jnp.where(chunk_o < 2, back, 0.0).astype(BF16), jnp.where(chunk_o < 2, 0.0, back).astype(BF16)]
    columns = jnp.concatenate(columns, axis=0)
    for w in range(waves):
        wave = dot(flipped[pl.ds(w * part_m, part_m), :], columns)
        send_c[w] = wave.astype(BF16).reshape(send_c.shape[1:])
        start_all(w, *stage_c)
    for w in range(waves):
        turned_ref[w] = leg[w].T
    store_turned = pltpu.make_async_copy(turned_ref, turned_hbm, store_sem.at[waves])
    store_turned.start()
    for w in range(waves):
        recv_all(w, *stage_c)
        swap(w, recv_c, send_d, nxz, group)
        start_all(w, *stage_d)

    stores = []
    for w in range(waves):
        recv_all(w, *stage_d)
        for yy in range(ny):
            parts = [recv_d[w, yy * nfld + ff].astype(F32) for ff in range(nfld)]
            for r in range(2):
                for j in range(2):
                    k = 2 * r + j
                    out = parts[0] if k == 0 else pltpu.roll(parts[0], (0 - k) % 4 * levels, 1)
                    for ff in range(1, nfld):
                        moved = parts[ff] if ff == k else pltpu.roll(parts[ff], (ff - k) % 4 * levels, 1)
                        out = jnp.where(chunk == ff, moved, out)
                    rows_f[pl.ds((r * waves + w) * lat + 2 * yy + j, nxz, stride=2 * ny), :] = out
        for r in range(2):
            rows = rows_f[pl.ds((r * waves + w) * lat, lat), :]
            wave_ref[w, :, pl.ds(r * lanes, lanes)] = rows.astype(BF16)
        stores.append(pltpu.make_async_copy(wave_ref.at[w], wave_hbm.at[w], store_sem.at[w]))
        stores[w].start()

    send_done(0, *obs_xz)
    send_done(0, *obs_y)
    for w in range(waves):
        for stage in (stage_a, stage_b, stage_c, stage_d):
            send_done(w, *stage)
    store_turned.wait()
    for store in stores:
        store.wait()


def on_device(coef, leg, vcoef, obs_value, obs_weight, obs_dest, obs_spot, obs_count, ny=NY):
    nblk = lax.axis_size("blk")
    nfld = lax.axis_size("fld")
    waves, lat, nn = leg.shape
    width = coef.shape[2]
    levels = vcoef.shape[2]
    lanes = 4 * levels
    nxz = nblk // ny
    group = ny * nfld
    part_m = nxz * group
    total_m = waves * part_m
    orows = nblk * SLOT_ROWS
    obs_dev = obs_spot.shape[0]

    def buffer(*shape):
        return pltpu.VMEM(shape, BF16)

    hbm = pl.BlockSpec(memory_space=pltpu.HBM)
    band_shape = (vcoef.shape[1], 1, levels)
    scratch = [
        buffer(waves, lat, width), buffer(waves, nn, lat),
        buffer(waves, lat, nn), buffer(waves, nn, width), pltpu.VMEM(band_shape, F32),
        buffer(levels, obs_dev), pltpu.VMEM((levels, obs_dev), F32), pltpu.VMEM((1, obs_dev), jnp.int32),
        pltpu.VMEM((1, obs_dev), jnp.int32), pltpu.VMEM((2 * waves * lat, lanes), F32),
        pltpu.VMEM((orows, lanes), F32),
        buffer(waves, group, nxz, lanes), buffer(waves, group, nxz, lanes),
        buffer(waves, nxz, group, lanes), buffer(waves, nxz, group, lanes),
        buffer(1, ny, nxz * SLOT_ROWS, lanes), buffer(1, ny, nxz * SLOT_ROWS, lanes),
        buffer(1, nxz, ny * SLOT_ROWS, lanes), buffer(1, nxz, ny * SLOT_ROWS, lanes),
        buffer(waves, nxz, group, lanes), buffer(waves, nxz, group, lanes),
        buffer(waves, group, nxz, lanes), buffer(waves, group, nxz, lanes),
        pltpu.VMEM((2, orows, lanes), F32), pltpu.VMEM((2, lanes, orows), F32),
        buffer(2, orows, 2 * total_m), buffer(total_m, 4 * orows),
        pltpu.SemaphoreType.DMA((7,)), pltpu.SemaphoreType.DMA((waves + 1,)),
    ]
    for parts in (waves, waves, 1, 1, waves, waves):
        scratch += [pltpu.SemaphoreType.DMA((parts,)), pltpu.SemaphoreType.DMA((parts,))]
    wave, turned = pl.pallas_call(
        functools.partial(kernel, nblk, nfld, ny),
        out_shape=(
            jax.ShapeDtypeStruct((waves, lat, width), BF16),
            jax.ShapeDtypeStruct((waves, nn, lat), BF16),
        ),
        in_specs=[hbm] * 7 + [pl.BlockSpec(memory_space=pltpu.SMEM)],
        out_specs=(hbm, hbm),
        scratch_shapes=scratch,
        compiler_params=pltpu.CompilerParams(
            collective_id=0, has_side_effects=True, vmem_limit_bytes=60 * 1024 * 1024
        ),
    )(
        leg, coef, vcoef.reshape(band_shape), obs_value[0], obs_weight[0], obs_dest.reshape(1, obs_dev),
        obs_spot.reshape(1, obs_dev), obs_count,
    )
    return jnp.einsum("mnj,mjc->mnc", turned, wave, preferred_element_type=F32).astype(BF16)


def solution(mesh):
    in_specs = (
        P(("blk", "fld"), None, None),
        P(("blk", "fld"), None, None),
        P("fld", None, None),
        P("fld", None, "blk"),
        P("fld", None, "blk"),
        P("blk", None),
        P("blk"),
        P("blk"),
    )
    out_specs = P(("blk", "fld"), None, None)
    return jax.shard_map(
        on_device, mesh=mesh, in_specs=in_specs, out_specs=out_specs, check_vma=False
    )
```

```python
import functools
import math

import jax
import jax.numpy as jnp
import numpy as np
from jax import lax
from jax.experimental import pallas as pl
from jax.experimental.pallas import tpu as pltpu
from jax.sharding import PartitionSpec as P

NLON = 2560
NY = 4
SLOT_ROWS = 4
MESH = pl.DeviceIdType.MESH
F32 = jnp.float32
BF16 = jnp.bfloat16


def power_series(f, terms):
    fit = np.polynomial.chebyshev.Chebyshev.interpolate(f, terms - 1, domain=[0.0, 0.25])
    return [float(c) for c in fit.convert(kind=np.polynomial.Polynomial).coef]


def cos_series():
    return power_series(lambda v: np.cos(2 * np.pi * np.sqrt(v)), 7)


def sin_series():
    return power_series(lambda v: 2 * np.pi * np.sinc(2 * np.sqrt(v)), 7)


def horner(coefs, v):
    total = jnp.full_like(v, coefs[-1])
    for c in coefs[-2::-1]:
        total = total * v + c
    return total


def cos_sin(turns, whole):
    rest = turns - jnp.round(turns * (1.0 / whole)) * whole
    u = rest * (1.0 / whole)
    v = u * u
    return horner(cos_series(), v), u * horner(sin_series(), v)


def dot(a, b, dims=(1, 0), precision=None):
    return lax.dot_general(
        a, b, (((dims[0],), (dims[1],)), ((), ())), precision=precision, preferred_element_type=F32
    )


def iota(shape, axis):
    return lax.broadcasted_iota(jnp.int32, shape, axis)


def kernel(
    nblk, nfld, ny, leg_hbm, coef_hbm, vcoef_hbm, val_hbm, wgt_hbm, dest_hbm, spot_hbm, count_ref, out_hbm,
    out, turned, leg, coef, vcoef_ref, val_ref, wgt_ref, dest_ref, spot_ref, rows_f, tmp_o, send_a, recv_a, send_b, recv_b, send_oa, recv_oa, send_ob, recv_ob,
    send_c, recv_c, send_d, recv_d, spot_col, spot_row, table, alpha, flipped,
    load_sem, store_sem, sa_s, sa_r, sb_s, sb_r, oa_s, oa_r, ob_s, ob_r, sc_s, sc_r, sd_s, sd_r,
):
    nxz = nblk // ny
    nz = nxz // 2
    group = ny * nfld
    waves, lat = leg.shape[0], leg.shape[1]
    part_m = nxz * group
    total_m = waves * part_m
    levels = vcoef_ref.shape[2]
    band = vcoef_ref.shape[0]
    half = (band - 1) // 2
    lanes = 4 * levels
    obs_dev = dest_ref.shape[1]
    orows = nblk * SLOT_ROWS
    slots = nblk * (SLOT_ROWS - 1)

    b = lax.axis_index("blk")
    f = lax.axis_index("fld")
    y = lax.rem(b, ny)
    xz = lax.div(b, ny)
    member = y * nfld + f

    x_hi = lax.div(xz, nz)
    z = lax.rem(xz, nz)

    def each_xz(act):
        for flip in (1, 0):
            plane = lax.rem(x_hi + flip, 2) * nz
            act(plane + lax.rem(z + nz // 2, nz))

            def step(i, carry):
                act(plane + lax.rem(z + nz // 2 - i, nz))
                act(plane + lax.rem(z + nz - nz // 2 + i, nz))
                return carry

            lax.fori_loop(1, nz // 2, step, 0)
            if flip:
                act(plane + z)

    def each_of(mine, count):
        def each(act):
            def step(i, carry):
                act(lax.rem(mine + i, count))
                return carry

            lax.fori_loop(1, count, step, 0)

        return each

    def group_device(mem):
        return (xz * ny + lax.div(mem, nfld), lax.rem(mem, nfld))

    def xz_device(other):
        return (other * ny + y, f)

    def y_device(other):
        return (xz * ny + other, f)

    def start_all(part, count, each, device, mine, src, dst, send_sem, recv_sem):
        def start(other):
            pltpu.make_async_remote_copy(
                src_ref=src.at[part, other], dst_ref=dst.at[part, mine], send_sem=send_sem.at[part],
                recv_sem=recv_sem.at[part], device_id=device(other), device_id_type=MESH,
            ).start()

        each(start)
        dst[part, mine] = src[part, mine]

    def whole(part, count, each, device, mine, src, dst, send_sem, recv_sem):
        others = pl.ds(0, count - 1)
        return pltpu.make_async_remote_copy(
            src_ref=src.at[part, others], dst_ref=dst.at[part, others], send_sem=send_sem.at[part],
            recv_sem=recv_sem.at[part], device_id=device(lax.rem(mine + 1, count)), device_id_type=MESH,
        )

    def recv_all(part, *stage):
        whole(part, *stage).wait_recv()

    def send_done(part, *stage):
        whole(part, *stage).wait_send()

    in_group = (group, each_of(member, group), group_device, member)
    in_xz = (nxz, each_xz, xz_device, xz)
    in_y = (ny, each_of(y, ny), y_device, y)
    stage_a = (*in_group, send_a, recv_a, sa_s, sa_r)
    stage_b = (*in_xz, send_b, recv_b, sb_s, sb_r)
    stage_c = (*in_xz, send_c, recv_c, sc_s, sc_r)
    stage_d = (*in_group, send_d, recv_d, sd_s, sd_r)
    obs_xz = (*in_xz, send_ob, recv_ob, ob_s, ob_r)
    obs_y = (*in_y, send_oa, recv_oa, oa_s, oa_r)

    loads = [
        pltpu.make_async_copy(src, dst, load_sem.at[i])
        for i, (src, dst) in enumerate(
            (
                (dest_hbm, dest_ref), (spot_hbm, spot_ref), (val_hbm, val_ref), (wgt_hbm, wgt_ref),
                (vcoef_hbm, vcoef_ref), (coef_hbm, coef), (leg_hbm, leg),
            )
        )
    ]
    for load in loads:
        load.start()
    barrier = pltpu.get_barrier_semaphore()

    def greet(count, each, device, mine):
        def tell(other):
            pl.semaphore_signal(barrier, inc=1, device_id=device(other), device_id_type=MESH)

        each(tell)

    greet(*in_xz)
    greet(*in_group)
    for load in loads[:5]:
        load.wait()

    dest = dest_ref[...]
    spot = spot_ref[...]
    live = iota((1, obs_dev), 1) < count_ref[0]
    place = jnp.where(live, lax.rem(dest, ny) * nxz + lax.div(dest, ny), -1)
    onehot = (iota((nblk, obs_dev), 0) == place).astype(BF16)
    part = min(128, obs_dev)
    upto = iota((part, 2 * part), 0) < iota((part, 2 * part), 1)
    ranks = []
    carry = jnp.zeros((nblk, part), F32)
    for i in range(obs_dev // part):
        piece = onehot[:, i * part : (i + 1) * part]
        counted = dot(piece, upto.astype(BF16))
        ranks.append(jnp.sum((counted[:, :part] + carry) * piece.astype(F32), axis=0, keepdims=True))
        carry = carry + counted[:, part:]
    rank = jnp.concatenate(ranks, axis=1).astype(jnp.int32)
    data = jnp.concatenate([val_ref[...].astype(F32), wgt_ref[...]], axis=0)
    lane_q = iota((lanes, obs_dev), 0)
    high = lax.div(spot, 32)
    low = spot - high * 32
    spots = jnp.where(lane_q == rank, high, jnp.where(lane_q == rank + 8, low, 0)).astype(F32)
    for k in range(SLOT_ROWS):
        rows = spots
        if k < SLOT_ROWS - 1:
            rows = [jnp.where(rank == 2 * k + h, data, 0.0) for h in range(2)]
            rows = jnp.concatenate(rows, axis=0)
        packed = dot(onehot, rows.astype(BF16), (1, 1))
        for yy in range(ny):
            tmp_o[pl.ds(yy * SLOT_ROWS + k, nxz, stride=ny * SLOT_ROWS), :] = packed[yy * nxz : (yy + 1) * nxz]
    send_ob[...] = tmp_o[...].astype(BF16).reshape(send_ob.shape)

    chunk = lax.div(iota((nxz, lanes), 1), levels)

    def pack(j):
        for yy in range(ny):
            parts = [
                rows_f[pl.ds((r * waves + w) * lat + 2 * yy + j, nxz, stride=2 * ny), :]
                for w in range(waves)
                for r in range(2)
            ]
            for ff in range(nfld):
                merged = parts[0] if ff == 0 else pltpu.roll(parts[0], (0 - ff) % 4 * levels, 1)
                for k in range(1, 4):
                    moved = parts[k] if ff == k else pltpu.roll(parts[k], (k - ff) % 4 * levels, 1)
                    merged = jnp.where(chunk == k, moved, merged)
                send_a[j, yy * nfld + ff] = merged.astype(BF16)

    def swap(part, src, dst, outer, inner):
        tmp_o[...] = src[part].astype(F32).reshape(tmp_o.shape)
        per = dst.shape[2] // outer
        for i in range(inner):
            rows = tmp_o[pl.ds(i, outer, stride=inner), :]
            dst[part, i // per, pl.ds(i % per * outer, outer), :] = rows.astype(BF16)

    for load in loads[5:]:
        load.wait()
    for w in range(waves):
        result = dot(leg[w], coef[w])
        for r in range(2):
            rows_f[pl.ds((r * waves + w) * lat, lat), :] = result[:, r * lanes : (r + 1) * lanes]
    pack(0)
    pl.semaphore_wait(barrier, group - 1 + nxz - 1)
    start_all(0, *stage_a)
    start_all(0, *obs_xz)
    pack(1)
    start_all(1, *stage_a)

    for j in range(2):
        recv_all(j, *stage_a)
        swap(j, recv_a, send_b, group, nxz)
        start_all(j, *stage_b)

    recv_all(0, *obs_xz)
    swap(0, recv_ob, send_oa, nxz, ny * SLOT_ROWS)
    start_all(0, *obs_y)
    recv_all(0, *obs_y)

    got = [recv_oa[0, yy, pl.ds(0, (SLOT_ROWS - 1) * nxz), :] for yy in range(ny)]
    got = jnp.concatenate(got, axis=0)
    spread = [recv_oa[0, yy, pl.ds((SLOT_ROWS - 1) * nxz, nxz), :] for yy in range(ny) for k in range(SLOT_ROWS - 1)]
    spread = jnp.concatenate(spread, axis=0).astype(F32)
    lane = iota((slots, lanes), 1)
    k_row = lax.rem(lax.div(iota((slots, lanes), 0), nxz), SLOT_ROWS - 1)
    for h in range(2):
        q = 2 * k_row + h
        mine = jnp.where(lane == q, spread * 32.0, jnp.where(lane == q + 8, spread, 0.0)).astype(BF16)
        spot_col[h] = dot(mine, jnp.ones((lanes, lanes), BF16))
        spot_row[h] = dot(jnp.ones((8, lanes), BF16), mine, (1, 1))

    def longitude(s):
        return jnp.where(s >= NLON, s - NLON, s)

    def turn(c, s, c1, s1):
        return c * c1 - s * s1, s * c1 + c * s1

    base = part_m // 4
    far = 2 * lanes
    tile = min(64, slots)
    for h in range(2):
        def along_m(i, carry):
            here = pl.ds(pl.multiple_of(i * tile, tile), tile)
            there = pl.ds(pl.multiple_of(h * slots + i * tile, tile), tile)
            lon = longitude(spot_col[h, here, :])
            for t in range(2):
                col = iota((tile, lanes), 1)
                step = lax.div(col, 2 * levels) + 2 * t
                quarter = lax.rem(lax.div(col, levels), 2) * (NLON // 4)
                phase = lon * (2 * base * step).astype(F32) - quarter.astype(F32)
                alpha[there, pl.ds(t * lanes, lanes)] = cos_sin(phase, NLON)[0]
            lon = lon[:, :base]
            odd = cos_sin(lon * (2 * iota((tile, base), 1) + 1).astype(F32), NLON)
            one = [jnp.broadcast_to(x[:, :1], x.shape) for x in odd]
            for w, pair in enumerate((turn(*odd, one[0], 0.0 - one[1]), odd)):
                for k in range(2):
                    table[there, pl.ds((2 * w + k) * base, base)] = pair[k].astype(BF16)
            return carry

        lax.fori_loop(0, slots // tile, along_m, 0)

    deep = min(64, base)
    wide = min(128, slots)
    for h in range(2):
        def along_o(i, carry):
            here = pl.ds(pl.multiple_of(i * wide, wide), wide)
            there = pl.ds(pl.multiple_of(h * slots + i * wide, wide), wide)
            lon = longitude(spot_row[h, :, here])
            one = [x[:1] for x in cos_sin(lon, NLON)]
            for q in range(base // deep):
                odd = cos_sin(lon[:1] * (2 * (iota((deep, wide), 0) + q * deep) + 1).astype(F32), NLON)
                for w, pair in enumerate((turn(*odd, one[0], 0.0 - one[1]), odd)):
                    for k in range(2):
                        flipped[pl.ds((2 * w + k) * base + q * deep, deep), there] = pair[k].astype(BF16)
            return carry

        lax.fori_loop(0, slots // wide, along_o, 0)

    scale = 1.0 / math.sqrt(total_m)
    vc = jnp.concatenate([vcoef_ref[:, 0, :]] * 4, axis=1) * scale
    lev_row = lax.rem(iota((lanes, lanes), 0), levels)
    lev_col = lax.rem(iota((lanes, lanes), 1), levels)
    up = jnp.zeros((lanes, lanes), F32)
    for k in range(band):
        up = up + jnp.where(lev_row == lev_col + (k - half), vc[k : k + 1, :], 0.0)
    col_chunk = lax.div(iota((lanes, lanes), 1), levels)
    ups = jnp.concatenate([jnp.where(col_chunk == 2 * h, up, 0.0) for h in (0, 0, 1, 1)], axis=0)
    chunk_o = lax.div(lane, levels)
    got32 = got.astype(F32)
    weight = pltpu.roll(got32, lanes - levels, 1)
    weight = jnp.where(lax.rem(chunk_o, 2) == 0, weight, 0.0)

    def split(x):
        coarse = x.astype(BF16)
        return coarse, (x - coarse.astype(F32)).astype(BF16)

    def dot3(a, split_b, dims):
        a0, a1 = split(a)
        b0, b1 = split_b
        return dot(a0, b0, dims) + (dot(a1, b0, dims) + dot(a0, b1, dims))

    ups = split(ups)
    latitude = jnp.where(chunk_o < 2, spot_col[0], spot_col[1]) >= NLON

    near_lane = iota((base, lanes), 1)
    low = near_lane < lanes // 2
    even = lax.rem(lax.div(near_lane, levels), 2) == 0

    for j in range(2):
        recv_all(j, *stage_b)
        four = recv_b[j].reshape(part_m, lanes).astype(F32)
        near = [four[a * base : (a + 1) * base] for a in range(4)]
        moved = [pltpu.roll(x, lanes // 2, 1) for x in near]
        sides = []
        for w in range(2):
            kept, other = (near, moved) if w == 0 else (moved, near)
            tops = [jnp.where(low, kept[2 * t], other[2 * t + 1]) for t in range(2)]
            sides.append(jnp.concatenate(tops, axis=1))
            crossed = [
                jnp.where(even, pltpu.roll(x, lanes - levels, 1), 0.0 - pltpu.roll(x, levels, 1)) for x in tops
            ]
            sides.append(jnp.concatenate(crossed, axis=1))
        grid = dot(table[...], jnp.concatenate(sides, axis=0).astype(BF16)) * alpha[...]
        grid = jnp.concatenate([grid[:slots], grid[slots:]], axis=1)
        here = latitude if j else jnp.logical_not(latitude)
        weighted = jnp.where(here, weight * (dot3(grid, ups, (1, 0)) - got32), 0.0)
        backs = dot3(weighted, ups, (1, 1))
        backs = jnp.concatenate([backs[:, :far], backs[:, far:]], axis=0) * alpha[...]
        sums = dot(flipped[...], backs.astype(BF16))
        mixed = []
        for w in range(2):
            by_cos, by_sin = [sums[(2 * w + k) * base : (2 * w + k + 1) * base] for k in range(2)]
            for t in range(2):
                x = by_sin[:, t * lanes : (t + 1) * lanes]
                x = jnp.where(even, 0.0 - pltpu.roll(x, lanes - levels, 1), pltpu.roll(x, levels, 1))
                mixed.append(by_cos[:, t * lanes : (t + 1) * lanes] + x)
        wave = []
        for t in range(2):
            first, second = mixed[t], mixed[2 + t]
            wave.append(jnp.where(low, first, pltpu.roll(second, lanes // 2, 1)))
            wave.append(jnp.where(low, pltpu.roll(first, lanes // 2, 1), second))
        wave = jnp.concatenate(wave, axis=0)
        send_c[j] = wave.astype(BF16).reshape(send_c.shape[1:])
        start_all(j, *stage_c)
        turned[j] = leg[j].T

    for j in range(2):
        recv_all(j, *stage_c)
        swap(j, recv_c, send_d, nxz, group)
        start_all(j, *stage_d)
    for j in range(2):
        recv_all(j, *stage_d)
        for yy in range(ny):
            parts = [recv_d[j, yy * nfld + ff].astype(F32) for ff in range(nfld)]
            for w in range(waves):
                for r in range(2):
                    k = 2 * w + r
                    merged = parts[0] if k == 0 else pltpu.roll(parts[0], (0 - k) % 4 * levels, 1)
                    for ff in range(1, nfld):
                        moved = parts[ff] if ff == k else pltpu.roll(parts[ff], (ff - k) % 4 * levels, 1)
                        merged = jnp.where(chunk == ff, moved, merged)
                    rows_f[pl.ds((r * waves + w) * lat + 2 * yy + j, nxz, stride=2 * ny), :] = merged
    stores = []
    for w in range(waves):
        wave = [rows_f[pl.ds((r * waves + w) * lat, lat), :].astype(BF16) for r in range(2)]
        out[w] = dot(turned[w], jnp.concatenate(wave, axis=1)).astype(BF16)
        stores.append(pltpu.make_async_copy(out.at[w], out_hbm.at[w], store_sem.at[w]))
        stores[w].start()

    send_done(0, *obs_xz)
    send_done(0, *obs_y)
    for j in range(2):
        for stage in (stage_a, stage_b, stage_c, stage_d):
            send_done(j, *stage)
    for store in stores:
        store.wait()


def on_device(coef, leg, vcoef, obs_value, obs_weight, obs_dest, obs_spot, obs_count, ny=NY):
    nblk = lax.axis_size("blk")
    nfld = lax.axis_size("fld")
    waves, lat, nn = leg.shape
    width = coef.shape[2]
    levels = vcoef.shape[2]
    lanes = 4 * levels
    nxz = nblk // ny
    group = ny * nfld
    part_m = nxz * group
    total_m = waves * part_m
    orows = nblk * SLOT_ROWS
    slots = nblk * (SLOT_ROWS - 1)
    obs_dev = obs_spot.shape[0]

    def buffer(*shape):
        return pltpu.VMEM(shape, BF16)

    hbm = pl.BlockSpec(memory_space=pltpu.HBM)
    band_shape = (vcoef.shape[1], 1, levels)
    scratch = [
        buffer(waves, nn, width), buffer(waves, nn, lat),
        buffer(waves, lat, nn), buffer(waves, nn, width), pltpu.VMEM(band_shape, F32),
        buffer(levels, obs_dev), pltpu.VMEM((levels, obs_dev), F32), pltpu.VMEM((1, obs_dev), jnp.int32),
        pltpu.VMEM((1, obs_dev), jnp.int32), pltpu.VMEM((2 * waves * lat, lanes), F32),
        pltpu.VMEM((orows, lanes), F32),
        buffer(2, group, nxz, lanes), buffer(2, group, nxz, lanes),
        buffer(2, nxz, group, lanes), buffer(2, nxz, group, lanes),
        buffer(1, ny, nxz * SLOT_ROWS, lanes), buffer(1, ny, nxz * SLOT_ROWS, lanes),
        buffer(1, nxz, ny * SLOT_ROWS, lanes), buffer(1, nxz, ny * SLOT_ROWS, lanes),
        buffer(2, nxz, group, lanes), buffer(2, nxz, group, lanes),
        buffer(2, group, nxz, lanes), buffer(2, group, nxz, lanes),
        pltpu.VMEM((2, slots, lanes), F32), pltpu.VMEM((2, 8, slots), F32),
        buffer(2 * slots, part_m), pltpu.VMEM((2 * slots, 2 * lanes), F32), buffer(part_m, 2 * slots),
        pltpu.SemaphoreType.DMA((7,)), pltpu.SemaphoreType.DMA((waves,)),
    ]
    for parts in (2, 2, 1, 1, 2, 2):
        scratch += [pltpu.SemaphoreType.DMA((parts,)), pltpu.SemaphoreType.DMA((parts,))]
    return pl.pallas_call(
        functools.partial(kernel, nblk, nfld, ny),
        out_shape=jax.ShapeDtypeStruct((waves, nn, width), BF16),
        in_specs=[hbm] * 7 + [pl.BlockSpec(memory_space=pltpu.SMEM)],
        out_specs=hbm,
        scratch_shapes=scratch,
        compiler_params=pltpu.CompilerParams(
            collective_id=0, has_side_effects=True, vmem_limit_bytes=60 * 1024 * 1024
        ),
    )(
        leg, coef, vcoef.reshape(band_shape), obs_value[0], obs_weight[0], obs_dest.reshape(1, obs_dev),
        obs_spot.reshape(1, obs_dev), obs_count,
    )

def solution(mesh):
    in_specs = (
        P(("blk", "fld"), None, None),
        P(("blk", "fld"), None, None),
        P("fld", None, None),
        P("fld", None, "blk"),
        P("fld", None, "blk"),
        P("blk", None),
        P("blk"),
        P("blk"),
    )
    out_specs = P(("blk", "fld"), None, None)
    return jax.shard_map(
        on_device, mesh=mesh, in_specs=in_specs, out_specs=out_specs, check_vma=False
    )
```

```python
import functools
import math

import jax
import jax.numpy as jnp
import numpy as np
from jax import lax
from jax.experimental import pallas as pl
from jax.experimental.pallas import tpu as pltpu
from jax.sharding import PartitionSpec as P

NLON = 2560
NY = 4
SLOT_ROWS = 4
MESH = pl.DeviceIdType.MESH
F32 = jnp.float32
BF16 = jnp.bfloat16


def power_series(f, terms):
    fit = np.polynomial.chebyshev.Chebyshev.interpolate(f, terms - 1, domain=[0.0, 0.25])
    return [float(c) for c in fit.convert(kind=np.polynomial.Polynomial).coef]


def cos_series():
    return power_series(lambda v: np.cos(2 * np.pi * np.sqrt(v)), 7)


def sin_series():
    return power_series(lambda v: 2 * np.pi * np.sinc(2 * np.sqrt(v)), 7)


def horner(coefs, v):
    total = jnp.full_like(v, coefs[-1])
    for c in coefs[-2::-1]:
        total = total * v + c
    return total


def cos_sin(turns, whole):
    rest = turns - jnp.round(turns * (1.0 / whole)) * whole
    u = rest * (1.0 / whole)
    v = u * u
    return horner(cos_series(), v), u * horner(sin_series(), v)


def dot(a, b, dims=(1, 0), precision=None):
    return lax.dot_general(
        a, b, (((dims[0],), (dims[1],)), ((), ())), precision=precision, preferred_element_type=F32
    )


def iota(shape, axis):
    return lax.broadcasted_iota(jnp.int32, shape, axis)


def kernel(
    nblk, nfld, ny, leg_hbm, coef_hbm, vcoef_hbm, val_hbm, wgt_hbm, dest_hbm, spot_hbm, count_ref, wave_hbm, turned_hbm,
    wave_ref, turned, leg, coef, vcoef_ref, val_ref, wgt_ref, dest_ref, spot_ref, rows_f, tmp_o, send_a, recv_a, send_b, recv_b, send_oa, recv_oa, send_ob, recv_ob,
    send_c, recv_c, send_d, recv_d, spot_col, spot_row, table, alpha, flipped,
    load_sem, store_sem, sa_s, sa_r, sb_s, sb_r, oa_s, oa_r, ob_s, ob_r, sc_s, sc_r, sd_s, sd_r,
):
    nxz = nblk // ny
    nz = nxz // 2
    group = ny * nfld
    waves, lat = leg.shape[0], leg.shape[1]
    part_m = nxz * group
    total_m = waves * part_m
    levels = vcoef_ref.shape[2]
    band = vcoef_ref.shape[0]
    half = (band - 1) // 2
    lanes = 4 * levels
    obs_dev = dest_ref.shape[1]
    orows = nblk * SLOT_ROWS
    slots = nblk * (SLOT_ROWS - 1)

    b = lax.axis_index("blk")
    f = lax.axis_index("fld")
    y = lax.rem(b, ny)
    xz = lax.div(b, ny)
    member = y * nfld + f

    x_hi = lax.div(xz, nz)
    z = lax.rem(xz, nz)

    def each_xz(act):
        for flip in (1, 0):
            plane = lax.rem(x_hi + flip, 2) * nz
            act(plane + lax.rem(z + nz // 2, nz))

            def step(i, carry):
                act(plane + lax.rem(z + nz // 2 - i, nz))
                act(plane + lax.rem(z + nz - nz // 2 + i, nz))
                return carry

            lax.fori_loop(1, nz // 2, step, 0)
            if flip:
                act(plane + z)

    def each_of(mine, count):
        def each(act):
            def step(i, carry):
                act(lax.rem(mine + i, count))
                return carry

            lax.fori_loop(1, count, step, 0)

        return each

    def group_device(mem):
        return (xz * ny + lax.div(mem, nfld), lax.rem(mem, nfld))

    def xz_device(other):
        return (other * ny + y, f)

    def y_device(other):
        return (xz * ny + other, f)

    def start_all(part, count, each, device, mine, src, dst, send_sem, recv_sem):
        def start(other):
            pltpu.make_async_remote_copy(
                src_ref=src.at[part, other], dst_ref=dst.at[part, mine], send_sem=send_sem.at[part],
                recv_sem=recv_sem.at[part], device_id=device(other), device_id_type=MESH,
            ).start()

        each(start)
        dst[part, mine] = src[part, mine]

    def whole(part, count, each, device, mine, src, dst, send_sem, recv_sem):
        others = pl.ds(0, count - 1)
        return pltpu.make_async_remote_copy(
            src_ref=src.at[part, others], dst_ref=dst.at[part, others], send_sem=send_sem.at[part],
            recv_sem=recv_sem.at[part], device_id=device(lax.rem(mine + 1, count)), device_id_type=MESH,
        )

    def recv_all(part, *stage):
        whole(part, *stage).wait_recv()

    def send_done(part, *stage):
        whole(part, *stage).wait_send()

    in_group = (group, each_of(member, group), group_device, member)
    in_xz = (nxz, each_xz, xz_device, xz)
    in_y = (ny, each_of(y, ny), y_device, y)
    stage_a = (*in_group, send_a, recv_a, sa_s, sa_r)
    stage_b = (*in_xz, send_b, recv_b, sb_s, sb_r)
    stage_c = (*in_xz, send_c, recv_c, sc_s, sc_r)
    stage_d = (*in_group, send_d, recv_d, sd_s, sd_r)
    obs_xz = (*in_xz, send_ob, recv_ob, ob_s, ob_r)
    obs_y = (*in_y, send_oa, recv_oa, oa_s, oa_r)

    loads = [
        pltpu.make_async_copy(src, dst, load_sem.at[i])
        for i, (src, dst) in enumerate(
            (
                (dest_hbm, dest_ref), (spot_hbm, spot_ref), (val_hbm, val_ref), (wgt_hbm, wgt_ref),
                (vcoef_hbm, vcoef_ref), (coef_hbm, coef), (leg_hbm, leg),
            )
        )
    ]
    barrier = pltpu.get_barrier_semaphore()

    def tell(device, other):
        pl.semaphore_signal(barrier, inc=1, device_id=device(other), device_id_type=MESH)

    for load in loads[5:]:
        load.start()
    for flip in (1, 0):
        for i in range(nz):
            if flip or i < nz - 1:
                move = (nz // 2 + (i + 1) // 2 * (1 if i % 2 else -1)) % nz
                tell(xz_device, lax.rem(x_hi + flip, 2) * nz + lax.rem(z + move, nz))
    for i in range(1, group):
        tell(group_device, lax.rem(member + i, group))
    for load in loads[:5]:
        load.start()
    for load in loads[:5]:
        load.wait()

    dest = dest_ref[...]
    spot = spot_ref[...]
    live = iota((1, obs_dev), 1) < count_ref[0]
    place = jnp.where(live, lax.rem(dest, ny) * nxz + lax.div(dest, ny), -1)
    onehot = (iota((nblk, obs_dev), 0) == place).astype(BF16)
    part = min(128, obs_dev)
    upto = iota((part, 2 * part), 0) < iota((part, 2 * part), 1)
    ranks = []
    carry = jnp.zeros((nblk, part), F32)
    for i in range(obs_dev // part):
        piece = onehot[:, i * part : (i + 1) * part]
        counted = dot(piece, upto.astype(BF16))
        ranks.append(jnp.sum((counted[:, :part] + carry) * piece.astype(F32), axis=0, keepdims=True))
        carry = carry + counted[:, part:]
    rank = jnp.concatenate(ranks, axis=1).astype(jnp.int32)
    data = jnp.concatenate([val_ref[...].astype(F32), wgt_ref[...]], axis=0)
    lane_q = iota((lanes, obs_dev), 0)
    high = lax.div(spot, 32)
    low = spot - high * 32
    spots = jnp.where(lane_q == rank, high, jnp.where(lane_q == rank + 8, low, 0)).astype(F32)
    for k in range(SLOT_ROWS):
        rows = spots
        if k < SLOT_ROWS - 1:
            rows = [jnp.where(rank == 2 * k + h, data, 0.0) for h in range(2)]
            rows = jnp.concatenate(rows, axis=0)
        packed = dot(onehot, rows.astype(BF16), (1, 1))
        for yy in range(ny):
            tmp_o[pl.ds(yy * SLOT_ROWS + k, nxz, stride=ny * SLOT_ROWS), :] = packed[yy * nxz : (yy + 1) * nxz]
    send_ob[...] = tmp_o[...].astype(BF16).reshape(send_ob.shape)

    chunk = lax.div(iota((nxz, lanes), 1), levels)

    def pack(j):
        for yy in range(ny):
            parts = [
                rows_f[pl.ds((r * waves + w) * lat + 2 * yy + j, nxz, stride=2 * ny), :]
                for w in range(waves)
                for r in range(2)
            ]
            for ff in range(nfld):
                merged = parts[0] if ff == 0 else pltpu.roll(parts[0], (0 - ff) % 4 * levels, 1)
                for k in range(1, 4):
                    moved = parts[k] if ff == k else pltpu.roll(parts[k], (k - ff) % 4 * levels, 1)
                    merged = jnp.where(chunk == k, moved, merged)
                send_a[j, yy * nfld + ff] = merged.astype(BF16)

    def swap(part, src, dst, outer, inner):
        tmp_o[...] = src[part].astype(F32).reshape(tmp_o.shape)
        per = dst.shape[2] // outer
        for i in range(inner):
            rows = tmp_o[pl.ds(i, outer, stride=inner), :]
            dst[part, i // per, pl.ds(i % per * outer, outer), :] = rows.astype(BF16)

    for load in loads[5:]:
        load.wait()
    for w in range(waves):
        result = dot(leg[w], coef[w])
        for r in range(2):
            rows_f[pl.ds((r * waves + w) * lat, lat), :] = result[:, r * lanes : (r + 1) * lanes]
    pack(0)
    pl.semaphore_wait(barrier, group - 1 + nxz - 1)
    start_all(0, *stage_a)
    start_all(0, *obs_xz)
    pack(1)
    start_all(1, *stage_a)

    for j in range(2):
        recv_all(j, *stage_a)
        swap(j, recv_a, send_b, group, nxz)
        start_all(j, *stage_b)

    recv_all(0, *obs_xz)
    swap(0, recv_ob, send_oa, nxz, ny * SLOT_ROWS)
    start_all(0, *obs_y)
    recv_all(0, *obs_y)

    got = [recv_oa[0, yy, pl.ds(0, (SLOT_ROWS - 1) * nxz), :] for yy in range(ny)]
    got = jnp.concatenate(got, axis=0)
    spread = [recv_oa[0, yy, pl.ds((SLOT_ROWS - 1) * nxz, nxz), :] for yy in range(ny) for k in range(SLOT_ROWS - 1)]
    spread = jnp.concatenate(spread, axis=0).astype(F32)
    lane = iota((slots, lanes), 1)
    k_row = lax.rem(lax.div(iota((slots, lanes), 0), nxz), SLOT_ROWS - 1)
    for h in range(2):
        q = 2 * k_row + h
        mine = jnp.where(lane == q, spread * 32.0, jnp.where(lane == q + 8, spread, 0.0)).astype(BF16)
        spot_col[h] = dot(mine, jnp.ones((lanes, lanes), BF16))
        spot_row[h] = dot(jnp.ones((8, lanes), BF16), mine, (1, 1))

    def longitude(s):
        return jnp.where(s >= NLON, s - NLON, s)

    def turn(c, s, c1, s1):
        return c * c1 - s * s1, s * c1 + c * s1

    base = part_m // 4
    far = 2 * lanes
    tile = min(64, slots)
    for h in range(2):
        def along_m(i, carry):
            here = pl.ds(pl.multiple_of(i * tile, tile), tile)
            there = pl.ds(pl.multiple_of(h * slots + i * tile, tile), tile)
            lon = longitude(spot_col[h, here, :])
            for t in range(2):
                col = iota((tile, lanes), 1)
                step = lax.div(col, 2 * levels) + 2 * t
                quarter = lax.rem(lax.div(col, levels), 2) * (NLON // 4)
                phase = lon * (2 * base * step).astype(F32) - quarter.astype(F32)
                alpha[there, pl.ds(t * lanes, lanes)] = cos_sin(phase, NLON)[0]
            lon = lon[:, :base]
            odd = cos_sin(lon * (2 * iota((tile, base), 1) + 1).astype(F32), NLON)
            one = [jnp.broadcast_to(x[:, :1], x.shape) for x in odd]
            for w, pair in enumerate((turn(*odd, one[0], 0.0 - one[1]), odd)):
                for k in range(2):
                    table[there, pl.ds((2 * w + k) * base, base)] = pair[k].astype(BF16)
            return carry

        lax.fori_loop(0, slots // tile, along_m, 0)

    deep = min(64, base)
    wide = min(128, slots)
    for h in range(2):
        def along_o(i, carry):
            here = pl.ds(pl.multiple_of(i * wide, wide), wide)
            there = pl.ds(pl.multiple_of(h * slots + i * wide, wide), wide)
            lon = longitude(spot_row[h, :, here])
            one = [x[:1] for x in cos_sin(lon, NLON)]
            for q in range(base // deep):
                odd = cos_sin(lon[:1] * (2 * (iota((deep, wide), 0) + q * deep) + 1).astype(F32), NLON)
                for w, pair in enumerate((turn(*odd, one[0], 0.0 - one[1]), odd)):
                    for k in range(2):
                        flipped[pl.ds((2 * w + k) * base + q * deep, deep), there] = pair[k].astype(BF16)
            return carry

        lax.fori_loop(0, slots // wide, along_o, 0)

    scale = 1.0 / math.sqrt(total_m)
    vc = jnp.concatenate([vcoef_ref[:, 0, :]] * 4, axis=1) * scale
    lev_row = lax.rem(iota((lanes, lanes), 0), levels)
    lev_col = lax.rem(iota((lanes, lanes), 1), levels)
    up = jnp.zeros((lanes, lanes), F32)
    for k in range(band):
        up = up + jnp.where(lev_row == lev_col + (k - half), vc[k : k + 1, :], 0.0)
    col_chunk = lax.div(iota((lanes, lanes), 1), levels)
    ups = jnp.concatenate([jnp.where(col_chunk == 2 * h, up, 0.0) for h in (0, 0, 1, 1)], axis=0)
    chunk_o = lax.div(lane, levels)
    got32 = got.astype(F32)
    weight = pltpu.roll(got32, lanes - levels, 1)
    weight = jnp.where(lax.rem(chunk_o, 2) == 0, weight, 0.0)

    def split(x):
        coarse = x.astype(BF16)
        return coarse, (x - coarse.astype(F32)).astype(BF16)

    def dot3(a, split_b, dims):
        a0, a1 = split(a)
        b0, b1 = split_b
        return dot(a0, b0, dims) + (dot(a1, b0, dims) + dot(a0, b1, dims))

    ups = split(ups)
    latitude = jnp.where(chunk_o < 2, spot_col[0], spot_col[1]) >= NLON

    near_lane = iota((base, lanes), 1)
    low = near_lane < lanes // 2
    even = lax.rem(lax.div(near_lane, levels), 2) == 0

    stores = []
    for j in range(2):
        recv_all(j, *stage_b)
        four = recv_b[j].reshape(part_m, lanes).astype(F32)
        near = [four[a * base : (a + 1) * base] for a in range(4)]
        moved = [pltpu.roll(x, lanes // 2, 1) for x in near]
        sides = []
        for w in range(2):
            kept, other = (near, moved) if w == 0 else (moved, near)
            tops = [jnp.where(low, kept[2 * t], other[2 * t + 1]) for t in range(2)]
            sides.append(jnp.concatenate(tops, axis=1))
            crossed = [
                jnp.where(even, pltpu.roll(x, lanes - levels, 1), 0.0 - pltpu.roll(x, levels, 1)) for x in tops
            ]
            sides.append(jnp.concatenate(crossed, axis=1))
        grid = dot(table[...], jnp.concatenate(sides, axis=0).astype(BF16)) * alpha[...]
        grid = jnp.concatenate([grid[:slots], grid[slots:]], axis=1)
        here = latitude if j else jnp.logical_not(latitude)
        weighted = jnp.where(here, weight * (dot3(grid, ups, (1, 0)) - got32), 0.0)
        backs = dot3(weighted, ups, (1, 1))
        backs = jnp.concatenate([backs[:, :far], backs[:, far:]], axis=0) * alpha[...]
        sums = dot(flipped[...], backs.astype(BF16))
        mixed = []
        for w in range(2):
            by_cos, by_sin = [sums[(2 * w + k) * base : (2 * w + k + 1) * base] for k in range(2)]
            for t in range(2):
                x = by_sin[:, t * lanes : (t + 1) * lanes]
                x = jnp.where(even, 0.0 - pltpu.roll(x, lanes - levels, 1), pltpu.roll(x, levels, 1))
                mixed.append(by_cos[:, t * lanes : (t + 1) * lanes] + x)
        wave = []
        for t in range(2):
            first, second = mixed[t], mixed[2 + t]
            wave.append(jnp.where(low, first, pltpu.roll(second, lanes // 2, 1)))
            wave.append(jnp.where(low, pltpu.roll(first, lanes // 2, 1), second))
        wave = jnp.concatenate(wave, axis=0)
        send_c[j] = wave.astype(BF16).reshape(send_c.shape[1:])
        start_all(j, *stage_c)
        turned[j] = leg[j].T
        stores.append(pltpu.make_async_copy(turned.at[j], turned_hbm.at[j], store_sem.at[j]))
        stores[j].start()

    for j in range(2):
        recv_all(j, *stage_c)
        swap(j, recv_c, send_d, nxz, group)
        start_all(j, *stage_d)
    for j in range(2):
        recv_all(j, *stage_d)
        for yy in range(ny):
            parts = [recv_d[j, yy * nfld + ff].astype(F32) for ff in range(nfld)]
            for w in range(waves):
                for r in range(2):
                    k = 2 * w + r
                    merged = parts[0] if k == 0 else pltpu.roll(parts[0], (0 - k) % 4 * levels, 1)
                    for ff in range(1, nfld):
                        moved = parts[ff] if ff == k else pltpu.roll(parts[ff], (ff - k) % 4 * levels, 1)
                        merged = jnp.where(chunk == ff, moved, merged)
                    rows_f[pl.ds((r * waves + w) * lat + 2 * yy + j, nxz, stride=2 * ny), :] = merged
    for w in range(waves):
        for r in range(2):
            rows = rows_f[pl.ds((r * waves + w) * lat, lat), :]
            wave_ref[w, :, pl.ds(r * lanes, lanes)] = rows.astype(BF16)
        stores.append(pltpu.make_async_copy(wave_ref.at[w], wave_hbm.at[w], store_sem.at[waves + w]))
        stores[waves + w].start()

    send_done(0, *obs_xz)
    send_done(0, *obs_y)
    for j in range(2):
        for stage in (stage_a, stage_b, stage_c, stage_d):
            send_done(j, *stage)
    for store in stores:
        store.wait()


def finish(cuts, wave_hbm, turned_hbm, out_hbm, wave, turned, out, wave_sem, load_sem, store_sem):
    waves, nn = turned.shape[0], turned.shape[1]
    size = nn // cuts
    wave_loads, loads, stores = [], [], []
    for w in range(waves):
        wave_loads.append(pltpu.make_async_copy(wave_hbm.at[w], wave.at[w], wave_sem.at[w]))
        wave_loads[w].start()
        for c in range(cuts):
            i, rows = w * cuts + c, pl.ds(c * size, size)
            loads.append(pltpu.make_async_copy(turned_hbm.at[w, rows], turned.at[w, rows], load_sem.at[i]))
            stores.append(pltpu.make_async_copy(out.at[w, rows], out_hbm.at[w, rows], store_sem.at[i]))
            loads[i].start()
    for w in range(waves):
        wave_loads[w].wait()
        for c in range(cuts):
            i, rows = w * cuts + c, pl.ds(c * size, size)
            loads[i].wait()
            out[w, rows] = dot(turned[w, rows], wave[w]).astype(BF16)
            stores[i].start()
    for store in stores:
        store.wait()


def on_device(coef, leg, vcoef, obs_value, obs_weight, obs_dest, obs_spot, obs_count, ny=NY):
    nblk = lax.axis_size("blk")
    nfld = lax.axis_size("fld")
    waves, lat, nn = leg.shape
    width = coef.shape[2]
    levels = vcoef.shape[2]
    lanes = 4 * levels
    nxz = nblk // ny
    group = ny * nfld
    part_m = nxz * group
    total_m = waves * part_m
    orows = nblk * SLOT_ROWS
    slots = nblk * (SLOT_ROWS - 1)
    obs_dev = obs_spot.shape[0]

    def buffer(*shape):
        return pltpu.VMEM(shape, BF16)

    hbm = pl.BlockSpec(memory_space=pltpu.HBM)
    band_shape = (vcoef.shape[1], 1, levels)
    scratch = [
        buffer(waves, lat, width), buffer(waves, nn, lat),
        buffer(waves, lat, nn), buffer(waves, nn, width), pltpu.VMEM(band_shape, F32),
        buffer(levels, obs_dev), pltpu.VMEM((levels, obs_dev), F32), pltpu.VMEM((1, obs_dev), jnp.int32),
        pltpu.VMEM((1, obs_dev), jnp.int32), pltpu.VMEM((2 * waves * lat, lanes), F32),
        pltpu.VMEM((orows, lanes), F32),
        buffer(2, group, nxz, lanes), buffer(2, group, nxz, lanes),
        buffer(2, nxz, group, lanes), buffer(2, nxz, group, lanes),
        buffer(1, ny, nxz * SLOT_ROWS, lanes), buffer(1, ny, nxz * SLOT_ROWS, lanes),
        buffer(1, nxz, ny * SLOT_ROWS, lanes), buffer(1, nxz, ny * SLOT_ROWS, lanes),
        buffer(2, nxz, group, lanes), buffer(2, nxz, group, lanes),
        buffer(2, group, nxz, lanes), buffer(2, group, nxz, lanes),
        pltpu.VMEM((2, slots, lanes), F32), pltpu.VMEM((2, 8, slots), F32),
        buffer(2 * slots, part_m), pltpu.VMEM((2 * slots, 2 * lanes), F32), buffer(part_m, 2 * slots),
        pltpu.SemaphoreType.DMA((7,)), pltpu.SemaphoreType.DMA((2 * waves,)),
    ]
    for parts in (2, 2, 1, 1, 2, 2):
        scratch += [pltpu.SemaphoreType.DMA((parts,)), pltpu.SemaphoreType.DMA((parts,))]
    wave, turned = pl.pallas_call(
        functools.partial(kernel, nblk, nfld, ny),
        out_shape=(
            jax.ShapeDtypeStruct((waves, lat, width), BF16),
            jax.ShapeDtypeStruct((waves, nn, lat), BF16),
        ),
        in_specs=[hbm] * 7 + [pl.BlockSpec(memory_space=pltpu.SMEM)],
        out_specs=(hbm, hbm),
        scratch_shapes=scratch,
        compiler_params=pltpu.CompilerParams(
            collective_id=0, has_side_effects=True, vmem_limit_bytes=60 * 1024 * 1024
        ),
    )(
        leg, coef, vcoef.reshape(band_shape), obs_value[0], obs_weight[0], obs_dest.reshape(1, obs_dev),
        obs_spot.reshape(1, obs_dev), obs_count,
    )
    cuts = 2
    return pl.pallas_call(
        functools.partial(finish, cuts),
        out_shape=jax.ShapeDtypeStruct((waves, nn, width), BF16),
        in_specs=[hbm, hbm],
        out_specs=hbm,
        scratch_shapes=[
            buffer(waves, lat, width), buffer(waves, nn, lat), buffer(waves, nn, width),
            pltpu.SemaphoreType.DMA((waves,)), pltpu.SemaphoreType.DMA((waves * cuts,)),
            pltpu.SemaphoreType.DMA((waves * cuts,)),
        ],
        compiler_params=pltpu.CompilerParams(vmem_limit_bytes=60 * 1024 * 1024),
    )(wave, turned)


def solution(mesh):
    in_specs = (
        P(("blk", "fld"), None, None),
        P(("blk", "fld"), None, None),
        P("fld", None, None),
        P("fld", None, "blk"),
        P("fld", None, "blk"),
        P("blk", None),
        P("blk"),
        P("blk"),
    )
    out_specs = P(("blk", "fld"), None, None)
    return jax.shard_map(
        on_device, mesh=mesh, in_specs=in_specs, out_specs=out_specs, check_vma=False
    )
```
